1024 devices in a mesh: gx: 64 (over x, z_hi, core), gy: 16 (over y, z_lo).
Axes of the slice: x: 8, y: 8, z: 8 (z_hi: 4, z_lo: 2; z = z_hi * 2 + z_lo), core: 2. Of those that a mesh axis runs over, the one named last changes fastest.
Arguments:
- inputs: bfloat16 [384, 8192], P(None, 'gx'), may hold values from -6 to 6
- grad_out: bfloat16 [384, 8192], P(None, 'gx'), may hold values from -2 to 2
- w_in: bfloat16 [8192, 32768], P('gx', 'gy'), may hold values from -0.0625 to 0.0625
- w_out: bfloat16 [32768, 8192], P('gy', 'gx'), may hold values from -0.03125 to 0.03125
Outputs:
- grad_inputs: bfloat16 [384, 8192], P('gy', 'gx')
- grad_w_in: float32 [8192, 32768], P('gx', 'gy')
- grad_w_out: float32 [32768, 8192], P('gy', 'gx')
The draws below stay inside these ranges and needn't reach their ends.
All inputs are finite; a program needn't handle non-finite values.
Results may differ from the reference program's by a relative error of at most 0.0049.
Values may be sent and summed in bfloat16 or wider, within the bound.
No kernel may reach another device: no remote copies, remote signals or barrier semaphores. Data moves between devices by JAX's collectives and lax.ppermute only.
A program may use at most 64 MiB of HBM per device.

```python
import jax
import jax.numpy as jnp
from jax import lax

D = 8192
FF = 32768
TOKENS = 384


def shard_levels(key, shape, shards, low, largest):
    gain, own = 1.0, jax.random.fold_in(key, 6)
    for dim, parts in shards:
        heights = jnp.exp(jax.random.uniform(jax.random.fold_in(own, dim), (parts,), jnp.float32, low / len(shards), largest / len(shards)))
        gain = gain * jnp.repeat(heights, shape[dim] // parts).reshape([-1 if axis == dim else 1 for axis in range(len(shape))])
    return gain


def bell_draw(key, extent, scale, limit, split=(), kind=jnp.bfloat16):
    values = scale * jax.random.normal(key, extent, jnp.float32)
    if split:
        values = values * shard_levels(key, extent, split, -0.22, 0.18)
    return jnp.clip(values, -limit, limit).astype(kind)


def setup_inputs(seed: int = 0) -> dict:
    seeds = jax.random.split(jax.random.key(seed), 5)
    inputs = bell_draw(seeds[0], (TOKENS, D), 1.0, 6.0, ((1, 64),))
    grad_out = bell_draw(seeds[1], (TOKENS, D), 0.25, 2.0, ((1, 64),))
    w_in = bell_draw(seeds[2], (D, FF), D ** -0.5, 0.0625, ((0, 64), (1, 16)))
    w_out = bell_draw(seeds[3], (FF, D), FF ** -0.5, 0.03125, ((0, 16), (1, 64)))
    return dict(inputs=inputs, grad_out=grad_out, w_in=w_in, w_out=w_out)


def gelu_tanh(values):
    return jax.nn.gelu(values, approximate=True)

def activate(hidden_pre, grad_act):
    activation, pullback = jax.vjp(gelu_tanh, hidden_pre)
    grad_pre = pullback(grad_act)[0]
    return (activation.astype(jnp.bfloat16), grad_pre.astype(jnp.bfloat16))

def reference(inputs, grad_out, w_in, w_out):
    hidden_pre = jnp.dot(inputs, w_in, preferred_element_type=jnp.float32)
    grad_act = lax.dot_general(grad_out, w_out, (((1,), (1,)), ((), ())), preferred_element_type=jnp.float32)
    activation, grad_pre = activate(hidden_pre, grad_act)
    grad_w_out = lax.dot_general(activation, grad_out, (((0,), (0,)), ((), ())), preferred_element_type=jnp.float32)
    grad_w_in = lax.dot_general(inputs, grad_pre, (((0,), (0,)), ((), ())), preferred_element_type=jnp.float32)
    grad_inputs = lax.dot_general(grad_pre, w_in, (((1,), (1,)), ((), ())), preferred_element_type=jnp.float32).astype(jnp.bfloat16)
    return (grad_inputs, grad_w_in, grad_w_out)
```

```python
import functools

import jax
import jax.numpy as jnp
import numpy as np
from jax import lax
from jax.experimental import pallas as pl
from jax.experimental.pallas import tpu as pltpu
from jax.sharding import Mesh, PartitionSpec as P

F32, BF16 = jnp.float32, jnp.bfloat16
PARAMS = pltpu.CompilerParams(vmem_limit_bytes=40 * 1024 * 1024)
OTHER = ((0, 1), (1, 0))
T, B = 384, 128
N = 8


def call(body, outs, *operands):
    vmem = pl.BlockSpec(memory_space=pltpu.VMEM)
    return pl.pallas_call(
        body,
        out_shape=outs,
        in_specs=[vmem] * len(operands),
        out_specs=jax.tree.map(lambda _: vmem, outs),
        compiler_params=PARAMS,
    )(*operands)


def columns(core, j):
    return pl.ds(pl.multiple_of(core * (N * B) + j * B, B), B)


def dot(a, b, dims):
    return lax.dot_general(a, b, (dims, ((), ())), preferred_element_type=F32)


def pack_in(x, w, out):
    other = 1 - lax.axis_index("c")
    out[:T] = x[...]
    for j in range(N):
        out[T + j * B : T + (j + 1) * B] = w[:, columns(other, j)]


def pack_out(x, w, out):
    other = 1 - lax.axis_index("c")
    out[:T] = x[...]
    for j in range(N):
        out[T + j * B : T + (j + 1) * B] = w[columns(other, j), :]


def hidden_part(x, w, theirs, out):
    core = lax.axis_index("c")
    for j in range(N):
        out[j] = (
            dot(x[...], w[:, columns(core, j)], ((1,), (0,)))
            + dot(theirs[:T], theirs[T + j * B : T + (j + 1) * B], ((1,), (0,)))
        ).astype(BF16)


def grad_part(x, w, theirs, out):
    core = lax.axis_index("c")
    for j in range(N):
        out[j] = (
            dot(x[...], w[columns(core, j), :], ((1,), (1,)))
            + dot(theirs[:T], theirs[T + j * B : T + (j + 1) * B], ((1,), (1,)))
        ).astype(BF16)


def add_blocks(parts, out):
    total = parts[0].astype(F32)
    for j in range(1, parts.shape[0]):
        total = total + parts[j].astype(F32)
    out[...] = total


def activate(parts, act, slope):
    v = parts[0]
    for j in range(1, parts.shape[0]):
        v = v + parts[j]
    k = np.float32(np.sqrt(2 / np.pi))
    cube = np.float32(0.044715)
    t = jnp.tanh(k * (v + cube * (v * v * v)))
    a = (0.5 * v * (1.0 + t)).astype(BF16)
    slope[...] = 0.5 * (1.0 + t) + 0.5 * v * (1.0 - t * t) * (
        k * (1.0 + 3.0 * cube * (v * v))
    )
    for j in range(N):
        act[j] = a


def back(parts, slope, out):
    g = parts[0]
    for j in range(1, parts.shape[0]):
        g = g + parts[j]
    p = (g * slope[...]).astype(BF16)
    for j in range(N):
        out[j] = p


def weight_out(mine, theirs, x, out):
    core = lax.axis_index("c")
    for j in range(N):
        out[columns(core, j), :] = dot(mine[j], x[...], ((0,), (0,)))
        out[columns(1 - core, j), :] = dot(theirs[j], x[...], ((0,), (0,)))


def weight_in(mine, theirs, x, out):
    core = lax.axis_index("c")
    for j in range(N):
        out[:, columns(core, j)] = dot(x[...], mine[j], ((0,), (0,)))
        out[:, columns(1 - core, j)] = dot(x[...], theirs[j], ((0,), (0,)))


def input_part(mine, theirs, w, out):
    core = lax.axis_index("c")
    total = jnp.zeros((T, B), F32)
    for j in range(N):
        total += dot(mine[j], w[:, columns(core, j)], ((1,), (1,)))
        total += dot(theirs[j], w[:, columns(1 - core, j)], ((1,), (1,)))
    out[...] = total


def finish(parts, out):
    total = parts[0]
    for j in range(1, parts.shape[0]):
        total = total + parts[j]
    out[...] = total.astype(BF16)


def per_device(inputs, grad_out, w_in, w_out):
    s = jax.ShapeDtypeStruct
    blocks = s((N, T, B), BF16)
    swap = lambda v: lax.ppermute(v, "c", OTHER)
    over_x = lambda v: lax.all_to_all(v, "x", 0, 0, tiled=True)
    over_z = lambda v: lax.all_gather(v, "zh", axis=0, tiled=False)

    theirs_in = swap(call(pack_in, s((T + N * B, B), BF16), inputs, w_in))
    theirs_out = swap(call(pack_out, s((T + N * B, B), BF16), grad_out, w_out))
    hidden = over_x(call(hidden_part, blocks, inputs, w_in, theirs_in))
    grad = over_x(call(grad_part, blocks, grad_out, w_out, theirs_out))
    hidden = over_z(call(add_blocks, s((T, B), F32), hidden))
    act, slope = call(activate, (blocks, s((T, B), F32)), hidden)
    act = over_x(act)
    grad = over_z(call(add_blocks, s((T, B), F32), grad))
    pre = over_x(call(back, blocks, grad, slope))
    act_theirs = swap(act)
    grad_w_out = call(weight_out, s((2 * N * B, B), F32), act, act_theirs, grad_out)
    pre_theirs = swap(pre)
    part = call(input_part, s((T, B), F32), pre, pre_theirs, w_in)
    part = lax.all_to_all(
        part.reshape(16, T // 16, B), ("y", "zl"), 0, 0, tiled=True
    )
    grad_w_in = call(weight_in, s((B, 2 * N * B), F32), pre, pre_theirs, inputs)
    grad_inputs = call(finish, s((T // 16, B), BF16), part)
    return (grad_inputs, grad_w_in, grad_w_out)


def solution(mesh):
    fine = Mesh(mesh.devices.reshape(8, 4, 2, 8, 2), ("x", "zh", "c", "y", "zl"))
    gx, gy = ("x", "zh", "c"), ("y", "zl")
    return jax.shard_map(
        per_device,
        mesh=fine,
        in_specs=(P(None, gx), P(None, gx), P(gx, gy), P(gy, gx)),
        out_specs=(P(gy, gx), P(gx, gy), P(gy, gx)),
        check_vma=False,
    )
```

```python
import functools

import jax
import jax.numpy as jnp
import numpy as np
from jax import lax
from jax.experimental import pallas as pl
from jax.experimental.pallas import tpu as pltpu
from jax.sharding import Mesh, PartitionSpec as P

F32, BF16 = jnp.float32, jnp.bfloat16
PARAMS = pltpu.CompilerParams(vmem_limit_bytes=40 * 1024 * 1024)
OTHER = ((0, 1), (1, 0))
T, B = 384, 128
N = 8


def call(body, outs, *operands, unread=0):
    vmem, stay = (pl.BlockSpec(memory_space=m) for m in (pltpu.VMEM, pl.ANY))
    return pl.pallas_call(
        body,
        out_shape=outs,
        in_specs=[vmem] * (len(operands) - unread) + [stay] * unread,
        out_specs=jax.tree.map(lambda _: vmem, outs),
        compiler_params=PARAMS,
    )(*operands)


def columns(core, j):
    return pl.ds(pl.multiple_of(core * (N * B) + j * B, B), B)


def dot(a, b, dims):
    return lax.dot_general(a, b, (dims, ((), ())), preferred_element_type=F32)


def pack_in(x, w, out):
    other = 1 - lax.axis_index("c")
    out[:T] = x[...]
    for j in range(N):
        out[T + j * B : T + (j + 1) * B] = w[:, columns(other, j)]


def pack_out(x, w, out):
    other = 1 - lax.axis_index("c")
    out[:T] = x[...]
    for j in range(N):
        out[T + j * B : T + (j + 1) * B] = w[columns(other, j), :]


def hidden_part(x, w, theirs, out):
    core = lax.axis_index("c")
    for j in range(N):
        out[j] = (
            dot(x[...], w[:, columns(core, j)], ((1,), (0,)))
            + dot(theirs[:T], theirs[T + j * B : T + (j + 1) * B], ((1,), (0,)))
        ).astype(BF16)


def grad_part(x, w, theirs, out):
    core = lax.axis_index("c")
    for j in range(N):
        out[j] = (
            dot(x[...], w[columns(core, j), :], ((1,), (1,)))
            + dot(theirs[:T], theirs[T + j * B : T + (j + 1) * B], ((1,), (1,)))
        ).astype(BF16)


def add_blocks(parts, out, rounded):
    total = parts[0].astype(F32)
    for j in range(1, N):
        total = total + parts[j].astype(F32)
    out[...] = total
    rounded[...] = total.astype(BF16)


def add_all(own, others):
    total = own[...]
    for other in others:
        total = total + other[...].astype(F32)
    return total


def activate(own, p1, p2, p3, act, slope):
    v = add_all(own, (p1, p2, p3))
    k = np.float32(np.sqrt(2 / np.pi))
    cube = np.float32(0.044715)
    t = jnp.tanh(k * (v + cube * (v * v * v)))
    a = (0.5 * v * (1.0 + t)).astype(BF16)
    slope[...] = 0.5 * (1.0 + t) + 0.5 * v * (1.0 - t * t) * (
        k * (1.0 + 3.0 * cube * (v * v))
    )
    for j in range(N):
        act[j] = a


def back(own, p1, p2, p3, slope, after, out):
    p = (add_all(own, (p1, p2, p3)) * slope[...]).astype(BF16)
    for j in range(N):
        out[j] = p


def weight_out(mine, theirs, x, out):
    core = lax.axis_index("c")
    for j in range(N):
        out[columns(core, j), :] = dot(mine[j], x[...], ((0,), (0,)))
        out[columns(1 - core, j), :] = dot(theirs[j], x[...], ((0,), (0,)))


def weight_in(mine, theirs, x, out):
    core = lax.axis_index("c")
    for j in range(N):
        out[:, columns(core, j)] = dot(x[...], mine[j], ((0,), (0,)))
        out[:, columns(1 - core, j)] = dot(x[...], theirs[j], ((0,), (0,)))


def input_part(mine, theirs, w, out):
    core = lax.axis_index("c")
    total = jnp.zeros((T, B), F32)
    for j in range(N):
        total += dot(mine[j], w[:, columns(core, j)], ((1,), (1,)))
        total += dot(theirs[j], w[:, columns(1 - core, j)], ((1,), (1,)))
    out[...] = total


def finish(parts, out):
    total = parts[0]
    for j in range(1, parts.shape[0]):
        total = total + parts[j]
    out[...] = total.astype(BF16)


def per_device(inputs, grad_out, w_in, w_out):
    s = jax.ShapeDtypeStruct
    blocks = s((N, T, B), BF16)
    swap = lambda v: lax.ppermute(v, "c", OTHER)
    over_x = lambda v: lax.all_to_all(v, "x", 0, 0, tiled=True)

    def over_z(own):
        return own[0], *(
            lax.ppermute(own[1], "zh", [(i, (i + step) % 4) for i in range(4)])
            for step in (1, 3, 2)
        )

    theirs_in = swap(call(pack_in, s((T + N * B, B), BF16), inputs, w_in))
    theirs_out = swap(call(pack_out, s((T + N * B, B), BF16), grad_out, w_out))
    hidden = over_x(call(hidden_part, blocks, inputs, w_in, theirs_in))
    grad = over_x(call(grad_part, blocks, grad_out, w_out, theirs_out))
    summed = (s((T, B), F32), s((T, B), BF16))
    hidden = over_z(call(add_blocks, summed, hidden))
    act, slope = call(activate, (blocks, s((T, B), F32)), *hidden)
    act = over_x(act)
    grad = over_z(call(add_blocks, summed, grad))
    pre = over_x(call(back, blocks, *grad, slope, act, unread=1))
    act_theirs = swap(act)
    grad_w_out = call(weight_out, s((2 * N * B, B), F32), act, act_theirs, grad_out)
    pre_theirs = swap(pre)
    part = call(input_part, s((T, B), F32), pre, pre_theirs, w_in)
    part = lax.all_to_all(
        part.reshape(16, T // 16, B), ("y", "zl"), 0, 0, tiled=True
    )
    grad_w_in = call(weight_in, s((B, 2 * N * B), F32), pre, pre_theirs, inputs)
    grad_inputs = call(finish, s((T // 16, B), BF16), part)
    return (grad_inputs, grad_w_in, grad_w_out)


def solution(mesh):
    fine = Mesh(mesh.devices.reshape(8, 4, 2, 8, 2), ("x", "zh", "c", "y", "zl"))
    gx, gy = ("x", "zh", "c"), ("y", "zl")
    return jax.shard_map(
        per_device,
        mesh=fine,
        in_specs=(P(None, gx), P(None, gx), P(gx, gy), P(gy, gx)),
        out_specs=(P(gy, gx), P(gx, gy), P(gy, gx)),
        check_vma=False,
    )
```

```python
import jax
import jax.numpy as jnp
import numpy as np
from jax import lax
from jax.experimental import pallas as pl
from jax.experimental.pallas import tpu as pltpu
from jax.sharding import PartitionSpec as P

F32, BF16 = jnp.float32, jnp.bfloat16
PARAMS = pltpu.CompilerParams(vmem_limit_bytes=40 * 1024 * 1024)
T, B = 384, 128
X, Z, C = 8, 4, 2
Q = T // Z

at = lambda x, z, c: (x * Z + z) * C + c
FOURS = [[at(2 * a + b, z, 0) for a in range(4)] for b in range(2) for z in range(Z)]
FOURS += [[at(x, z, 1) for z in range(Z)] for x in range(X)]
EIGHTS = [[at(2 * a + b, z, 0) for b in range(2) for z in range(Z)] for a in range(4)]
EIGHTS += [[at(x, z, 1) for x in range(X)] for z in range(Z)]
SWAP = [(i, i ^ 1) for i in range(X * Z * C)]


def place(core, x, z):
    first = core == 0
    return jnp.where(first, x // 2, z), jnp.where(first, x % 2 * Z + z, x)


def call(body, outs, *operands):
    vmem = pl.BlockSpec(memory_space=pltpu.VMEM)
    return pl.pallas_call(
        body,
        out_shape=outs,
        in_specs=[vmem] * len(operands),
        out_specs=jax.tree.map(lambda _: vmem, outs),
        compiler_params=PARAMS,
    )(*operands)


def this_core():
    return lax.rem(lax.axis_index("gx"), C)


def columns(core, x):
    return pl.ds(pl.multiple_of((core * X + x) * B, B), B)


def dot(a, b, dims):
    return lax.dot_general(a, b, (dims, ((), ())), preferred_element_type=F32)


def pack(x, w_in, y, w_out, out):
    other = 1 - this_core()
    out[0, :T] = x[...]
    out[1, :T] = y[...]
    for j in range(X):
        rows = slice(T + j * B, T + (j + 1) * B)
        out[0, rows] = w_in[:, columns(other, j)]
        out[1, rows] = w_out[columns(other, j), :]


def partial_sums(x, w_in, y, w_out, theirs, out):
    core = this_core()
    for j in range(X):
        rows = slice(T + j * B, T + (j + 1) * B)
        h = dot(x[...], w_in[:, columns(core, j)], ((1,), (0,)))
        h = h + dot(theirs[0, :T], theirs[0, rows], ((1,), (0,)))
        g = dot(y[...], w_out[columns(core, j), :], ((1,), (1,)))
        g = g + dot(theirs[1, :T], theirs[1, rows], ((1,), (1,)))
        h, g = h.astype(BF16), g.astype(BF16)
        for z in range(Z):
            four, eight = place(core, j, z)
            out[four, eight, 0] = h[z * Q : (z + 1) * Q]
            out[four, eight, 1] = g[z * Q : (z + 1) * Q]


def total(parts):
    value = parts[0].astype(F32)
    for j in range(1, parts.shape[0]):
        value = value + parts[j].astype(F32)
    return value


def add_fours(parts, out):
    out[...] = total(parts).astype(BF16)


def middle(parts, out):
    both = total(parts)
    v, g = both[0], both[1]
    k = np.float32(np.sqrt(2 / np.pi))
    cube = np.float32(0.044715)
    t = jnp.tanh(k * (v + cube * (v * v * v)))
    act = (0.5 * v * (1.0 + t)).astype(BF16)
    slope = 0.5 * (1.0 + t) + 0.5 * v * (1.0 - t * t) * (
        k * (1.0 + 3.0 * cube * (v * v))
    )
    pre = (g * slope).astype(BF16)
    for j in range(X):
        out[j, 0] = act
        out[j, 1] = pre


def copies(part, out):
    for j in range(4):
        out[j] = part[...]


def tokens(ref, core, x, which):
    blocks = [ref[(*place(core, x, z), which)] for z in range(Z)]
    return jnp.concatenate(blocks, axis=0)


def input_part(mine, theirs, w, out):
    core = this_core()
    value = jnp.zeros((T, B), F32)
    for who, ref in ((core, mine), (1 - core, theirs)):
        for j in range(X):
            value += dot(tokens(ref, who, j, 1), w[:, columns(who, j)], ((1,), (1,)))
    out[...] = value


def weights(mine, theirs, x, y, out_in, out_out):
    core = this_core()
    for who, ref in ((core, mine), (1 - core, theirs)):
        for j in range(X):
            there = columns(who, j)
            out_in[:, there] = dot(x[...], tokens(ref, who, j, 1), ((0,), (0,)))
            out_out[there, :] = dot(tokens(ref, who, j, 0), y[...], ((0,), (0,)))


def finish(parts, out):
    out[...] = total(parts).astype(BF16)


def per_device(inputs, grad_out, w_in, w_out):
    s = jax.ShapeDtypeStruct
    swap = lambda v: lax.ppermute(v, "gx", SWAP)

    def exchange(v, groups):
        return lax.all_to_all(v, "gx", 0, 0, axis_index_groups=groups, tiled=True)

    both = (4, X, 2, Q, B)
    theirs = swap(call(pack, s((2, T + X * B, B), BF16), inputs, w_in, grad_out, w_out))
    sums = call(partial_sums, s(both, BF16), inputs, w_in, grad_out, w_out, theirs)
    sums = call(add_fours, s(both[1:], BF16), exchange(sums, FOURS))
    mine = call(middle, s(both[1:], BF16), exchange(sums, EIGHTS))
    mine = exchange(call(copies, s(both, BF16), exchange(mine, EIGHTS)), FOURS)
    theirs = swap(mine)
    part = call(input_part, s((T, B), F32), mine, theirs, w_in)
    part = lax.all_to_all(part.reshape(16, T // 16, B), "gy", 0, 0, tiled=True)
    outs = (s((B, 2 * X * B), F32), s((2 * X * B, B), F32))
    grad_w_in, grad_w_out = call(weights, outs, mine, theirs, inputs, grad_out)
    grad_inputs = call(finish, s((T // 16, B), BF16), part)
    return (grad_inputs, grad_w_in, grad_w_out)


def solution(mesh):
    return jax.shard_map(
        per_device,
        mesh=mesh,
        in_specs=(P(None, "gx"), P(None, "gx"), P("gx", "gy"), P("gy", "gx")),
        out_specs=(P("gy", "gx"), P("gx", "gy"), P("gy", "gx")),
        check_vma=False,
    )
```

```python
import jax
import jax.numpy as jnp
import numpy as np
from jax import lax
from jax.experimental import pallas as pl
from jax.experimental.pallas import tpu as pltpu
from jax.sharding import PartitionSpec as P

F32, BF16 = jnp.float32, jnp.bfloat16
PARAMS = pltpu.CompilerParams(vmem_limit_bytes=40 * 1024 * 1024)
T, B = 384, 128
X, Z, C = 8, 4, 2
Q = T // Z

at = lambda x, z, c: (x * Z + z) * C + c
EIGHTS = [[at(x, z, 0) for x in range(X)] for z in range(Z)]
EIGHTS += [[at(2 * a + b, z, 1) for b in range(2) for z in range(Z)] for a in range(4)]
FOURS = [[at(x, z, 0) for z in range(Z)] for x in range(X)]
FOURS += [[at(2 * a + b, z, 1) for a in range(4)] for b in range(2) for z in range(Z)]
SWAP = [(i, i ^ 1) for i in range(X * Z * C)]


def place(core, x, z):
    first = core == 0
    return jnp.where(first, x, x % 2 * Z + z), jnp.where(first, z, x // 2)


def call(body, outs, *operands):
    vmem = pl.BlockSpec(memory_space=pltpu.VMEM)
    return pl.pallas_call(
        body,
        out_shape=outs,
        in_specs=[vmem] * len(operands),
        out_specs=jax.tree.map(lambda _: vmem, outs),
        compiler_params=PARAMS,
    )(*operands)


def this_core():
    return lax.rem(lax.axis_index("gx"), C)


def columns(core, x):
    return pl.ds(pl.multiple_of((core * X + x) * B, B), B)


def dot(a, b, dims):
    return lax.dot_general(a, b, (dims, ((), ())), preferred_element_type=F32)


def pack(x, w_in, y, w_out, out):
    other = 1 - this_core()
    out[0, :T] = x[...]
    out[1, :T] = y[...]
    for j in range(X):
        rows = slice(T + j * B, T + (j + 1) * B)
        out[0, rows] = w_in[:, columns(other, j)]
        out[1, rows] = w_out[columns(other, j), :]


def partial_sums(x, w_in, y, w_out, theirs, out):
    core = this_core()
    for j in range(X):
        rows = slice(T + j * B, T + (j + 1) * B)
        h = dot(x[...], w_in[:, columns(core, j)], ((1,), (0,)))
        h = h + dot(theirs[0, :T], theirs[0, rows], ((1,), (0,)))
        g = dot(y[...], w_out[columns(core, j), :], ((1,), (1,)))
        g = g + dot(theirs[1, :T], theirs[1, rows], ((1,), (1,)))
        h, g = h.astype(BF16), g.astype(BF16)
        for z in range(Z):
            eight, four = place(core, j, z)
            out[eight, four, 0] = h[z * Q : (z + 1) * Q]
            out[eight, four, 1] = g[z * Q : (z + 1) * Q]


def total(parts):
    value = parts[0].astype(F32)
    for j in range(1, parts.shape[0]):
        value = value + parts[j].astype(F32)
    return value


def add_eights(parts, out):
    value = total(parts).astype(BF16)
    for j in range(4):
        out[j] = value


def middle(parts, out):
    both = total(parts)
    v, g = both[:, 0], both[:, 1]
    k = np.float32(np.sqrt(2 / np.pi))
    cube = np.float32(0.044715)
    t = jnp.tanh(k * (v + cube * (v * v * v)))
    act = (0.5 * v * (1.0 + t)).astype(BF16)
    slope = 0.5 * (1.0 + t) + 0.5 * v * (1.0 - t * t) * (
        k * (1.0 + 3.0 * cube * (v * v))
    )
    pre = (g * slope).astype(BF16)
    for j in range(8):
        out[j, :, 0] = act
        out[j, :, 1] = pre


def tokens(ref, core, x, which):
    blocks = [ref[(*place(core, x, z), which)] for z in range(Z)]
    return jnp.concatenate(blocks, axis=0)


def input_part(mine, theirs, w, out):
    core = this_core()
    value = jnp.zeros((T, B), F32)
    for who, ref in ((core, mine), (1 - core, theirs)):
        for j in range(X):
            value += dot(tokens(ref, who, j, 1), w[:, columns(who, j)], ((1,), (1,)))
    out[...] = value


def weights(mine, theirs, x, y, out_in, out_out):
    core = this_core()
    for who, ref in ((core, mine), (1 - core, theirs)):
        for j in range(X):
            there = columns(who, j)
            out_in[:, there] = dot(x[...], tokens(ref, who, j, 1), ((0,), (0,)))
            out_out[there, :] = dot(tokens(ref, who, j, 0), y[...], ((0,), (0,)))


def finish(parts, out):
    out[...] = total(parts).astype(BF16)


def per_device(inputs, grad_out, w_in, w_out):
    s = jax.ShapeDtypeStruct
    swap = lambda v: lax.ppermute(v, "gx", SWAP)

    def exchange(v, groups):
        return lax.all_to_all(v, "gx", 0, 0, axis_index_groups=groups, tiled=True)

    blocks = (4, 2, Q, B)
    theirs = swap(call(pack, s((2, T + X * B, B), BF16), inputs, w_in, grad_out, w_out))
    sums = call(partial_sums, s((8, *blocks), BF16), inputs, w_in, grad_out, w_out, theirs)
    sums = call(add_eights, s((4, *blocks), BF16), exchange(sums, EIGHTS))
    mine = call(middle, s((8, *blocks), BF16), exchange(sums, FOURS))
    mine = exchange(mine, EIGHTS)
    theirs = swap(mine)
    part = call(input_part, s((T, B), F32), mine, theirs, w_in)
    part = lax.all_to_all(part.reshape(16, T // 16, B), "gy", 0, 0, tiled=True)
    outs = (s((B, 2 * X * B), F32), s((2 * X * B, B), F32))
    grad_w_in, grad_w_out = call(weights, outs, mine, theirs, inputs, grad_out)
    grad_inputs = call(finish, s((T // 16, B), BF16), part)
    return (grad_inputs, grad_w_in, grad_w_out)


def solution(mesh):
    return jax.shard_map(
        per_device,
        mesh=mesh,
        in_specs=(P(None, "gx"), P(None, "gx"), P("gx", "gy"), P("gy", "gx")),
        out_specs=(P("gy", "gx"), P("gx", "gy"), P("gy", "gx")),
        check_vma=False,
    )
```

```python
import jax
import jax.numpy as jnp
import numpy as np
from jax import lax
from jax.experimental import pallas as pl
from jax.experimental.pallas import tpu as pltpu
from jax.sharding import PartitionSpec as P

F32, BF16 = jnp.float32, jnp.bfloat16
PARAMS = pltpu.CompilerParams(vmem_limit_bytes=40 * 1024 * 1024)
T, B = 384, 128
X, Z, C = 8, 4, 2
Q = T // Z

at = lambda x, z, c: (x * Z + z) * C + c
EIGHTS = [[at(x, z, 0) for x in range(X)] for z in range(Z)]
EIGHTS += [[at(2 * a + b, z, 1) for b in range(2) for z in range(Z)] for a in range(4)]
FOURS = [[at(x, z, 0) for z in range(Z)] for x in range(X)]
FOURS += [[at(2 * a + b, z, 1) for a in range(4)] for b in range(2) for z in range(Z)]
ROUND = [[(g[i], g[(i + s) % 4]) for g in FOURS for i in range(4)] for s in (1, 3, 2)]
SWAP = [(i, i ^ 1) for i in range(X * Z * C)]


def place(core, x, z):
    first = core == 0
    return jnp.where(first, x, x % 2 * Z + z), jnp.where(first, z, x // 2)


def call(body, outs, *operands, unread=0, where=pltpu.VMEM, scratch=()):
    vmem, stay = (pl.BlockSpec(memory_space=m) for m in (pltpu.VMEM, pl.ANY))
    read = pl.BlockSpec(memory_space=where)
    return pl.pallas_call(
        body,
        out_shape=outs,
        in_specs=[read] * (len(operands) - unread) + [stay] * unread,
        out_specs=jax.tree.map(lambda _: vmem, outs),
        scratch_shapes=scratch,
        compiler_params=PARAMS,
    )(*operands)


def this_core():
    return lax.rem(lax.axis_index("gx"), C)


def columns(core, x):
    return pl.ds(pl.multiple_of((core * X + x) * B, B), B)


def dot(a, b, dims):
    return lax.dot_general(a, b, (dims, ((), ())), preferred_element_type=F32)


def rows(x):
    return pl.ds(T + x * B, B)


def pack_in(x, w, out, sem):
    other = 1 - this_core()
    pairs = [(x, out.at[pl.ds(0, T)])]
    pairs += [(w.at[:, columns(other, j)], out.at[rows(j)]) for j in range(X)]
    move(pairs, sem)


def pack_out(x, w, out, sem):
    start = pl.multiple_of((1 - this_core()) * (X * B), B)
    pairs = [(x, out.at[pl.ds(0, T)])]
    pairs += [(w.at[pl.ds(start, X * B)], out.at[pl.ds(T, X * B)])]
    move(pairs, sem)


def move(pairs, sem):
    copies = [pltpu.make_async_copy(a, b, sem.at[i]) for i, (a, b) in enumerate(pairs)]
    for copy in copies:
        copy.start()
    for copy in copies:
        copy.wait()


def scatter(value, out, core, x):
    value = value.astype(BF16)
    for z in range(Z):
        eight, four = place(core, x, z)
        out[eight, four] = value[z * Q : (z + 1) * Q]


def hidden_part(x, w, theirs, out):
    core = this_core()
    for j in range(X):
        value = dot(x[...], w[:, columns(core, j)], ((1,), (0,)))
        value += dot(theirs[:T], theirs[rows(j)], ((1,), (0,)))
        scatter(value, out, core, j)


def grad_part(x, w, theirs, out):
    core = this_core()
    for j in range(X):
        value = dot(x[...], w[columns(core, j), :], ((1,), (1,)))
        value += dot(theirs[:T], theirs[rows(j)], ((1,), (1,)))
        scatter(value, out, core, j)


def total(parts):
    value = parts[0].astype(F32)
    for j in range(1, parts.shape[0]):
        value = value + parts[j].astype(F32)
    return value


def add_eight(parts, out, rounded):
    value = total(parts)
    out[...] = value
    rounded[...] = value.astype(BF16)


def add_four(own, others):
    value = own[...]
    for other in others:
        value = value + other[...].astype(F32)
    return value


def activate(own, p1, p2, p3, act, slope):
    v = add_four(own, (p1, p2, p3))
    k = np.float32(np.sqrt(2 / np.pi))
    cube = np.float32(0.044715)
    t = jnp.tanh(k * (v + cube * (v * v * v)))
    a = (0.5 * v * (1.0 + t)).astype(BF16)
    slope[...] = 0.5 * (1.0 + t) + 0.5 * v * (1.0 - t * t) * (
        k * (1.0 + 3.0 * cube * (v * v))
    )
    for j in range(8):
        act[j] = a


def back(own, p1, p2, p3, slope, after, out):
    p = (add_four(own, (p1, p2, p3)) * slope[...]).astype(BF16)
    for j in range(8):
        out[j] = p


def tokens(ref, core, x):
    return jnp.concatenate([ref[place(core, x, z)] for z in range(Z)], axis=0)


def weight_out(mine, theirs, x, out):
    core = this_core()
    for who, ref in ((core, mine), (1 - core, theirs)):
        for j in range(X):
            out[columns(who, j), :] = dot(tokens(ref, who, j), x[...], ((0,), (0,)))


def weight_in(mine, theirs, x, out):
    core = this_core()
    for who, ref in ((core, mine), (1 - core, theirs)):
        for j in range(X):
            out[:, columns(who, j)] = dot(x[...], tokens(ref, who, j), ((0,), (0,)))


def input_part(mine, theirs, w, out):
    core = this_core()
    value = jnp.zeros((T, B), F32)
    for who, ref in ((core, mine), (1 - core, theirs)):
        for j in range(X):
            value += dot(tokens(ref, who, j), w[:, columns(who, j)], ((1,), (1,)))
    out[...] = value


def finish(parts, out):
    out[...] = total(parts).astype(BF16)


def per_device(inputs, grad_out, w_in, w_out):
    s = jax.ShapeDtypeStruct
    four = (4, Q, B)
    eight = s((8, *four), BF16)
    packed = s((T + X * B, B), BF16)
    summed = (s(four, F32), s(four, BF16))
    swap = lambda v: lax.ppermute(v, "gx", SWAP)

    def exchange(v):
        return lax.all_to_all(v, "gx", 0, 0, axis_index_groups=EIGHTS, tiled=True)

    def around(own, rounded):
        return own, *(lax.ppermute(rounded, "gx", pairs) for pairs in ROUND)

    def packs(body, copies, x, w):
        sems = (pltpu.SemaphoreType.DMA((copies,)),)
        return swap(call(body, packed, x, w, where=pltpu.HBM, scratch=sems))

    theirs_in = packs(pack_in, 1 + X, inputs, w_in)
    theirs_out = packs(pack_out, 2, grad_out, w_out)
    hidden = exchange(call(hidden_part, eight, inputs, w_in, theirs_in))
    grad = exchange(call(grad_part, eight, grad_out, w_out, theirs_out))
    hidden = around(*call(add_eight, summed, hidden))
    act, slope = call(activate, (eight, s(four, F32)), *hidden)
    act = exchange(act)
    grad = around(*call(add_eight, summed, grad))
    pre = exchange(call(back, eight, *grad, slope, act, unread=1))
    act_theirs = swap(act)
    grad_w_out = call(weight_out, s((2 * X * B, B), F32), act, act_theirs, grad_out)
    pre_theirs = swap(pre)
    part = call(input_part, s((T, B), F32), pre, pre_theirs, w_in)
    part = lax.all_to_all(part.reshape(16, T // 16, B), "gy", 0, 0, tiled=True)
    grad_w_in = call(weight_in, s((B, 2 * X * B), F32), pre, pre_theirs, inputs)
    grad_inputs = call(finish, s((T // 16, B), BF16), part)
    return (grad_inputs, grad_w_in, grad_w_out)


def solution(mesh):
    return jax.shard_map(
        per_device,
        mesh=mesh,
        in_specs=(P(None, "gx"), P(None, "gx"), P("gx", "gy"), P("gy", "gx")),
        out_specs=(P("gy", "gx"), P("gx", "gy"), P("gy", "gx")),
        check_vma=False,
    )
```

```python
import jax
import jax.numpy as jnp
import numpy as np
from jax import lax
from jax.experimental import pallas as pl
from jax.experimental.pallas import tpu as pltpu
from jax.sharding import PartitionSpec as P

F32, BF16 = jnp.float32, jnp.bfloat16
PARAMS = pltpu.CompilerParams(vmem_limit_bytes=40 * 1024 * 1024)
T, B = 384, 128
X, Z, C = 8, 4, 2
Q = T // Z

at = lambda x, z, c: (x * Z + z) * C + c
fold = lambda a, b: a if b == 0 else X - 1 - a
FOURS = [[at(fold(a, b), z, 0) for a in range(4)] for b in range(2) for z in range(Z)]
FOURS += [[at(x, z, 1) for z in range(Z)] for x in range(X)]
EIGHTS = [[at(fold(a, b), z, 0) for b in range(2) for z in range(Z)] for a in range(4)]
EIGHTS += [[at(x, z, 1) for x in range(X)] for z in range(Z)]
SWAP = [(i, i ^ 1) for i in range(X * Z * C)]


def place(core, x, z):
    first = core == 0
    return jnp.where(first, min(x, X - 1 - x), z), jnp.where(first, x // 4 * Z + z, x)


def call(body, outs, *operands, where=pltpu.VMEM, params=PARAMS, scratch=()):
    vmem, read = (pl.BlockSpec(memory_space=m) for m in (pltpu.VMEM, where))
    return pl.pallas_call(
        body,
        out_shape=outs,
        in_specs=[read] * len(operands),
        out_specs=jax.tree.map(lambda _: vmem, outs),
        scratch_shapes=scratch,
        compiler_params=params,
    )(*operands)


def this_core():
    return lax.rem(lax.axis_index("gx"), C)


def columns(core, x):
    return pl.ds(pl.multiple_of((core * X + x) * B, B), B)


def dot(a, b, dims):
    return lax.dot_general(a, b, (dims, ((), ())), preferred_element_type=F32)


def pack(x, w_in, y, w_out, out, sem):
    other = 1 - this_core()
    half = pl.ds(pl.multiple_of(other * X * B, B), X * B)
    pairs = [(x, out.at[0, pl.ds(0, T)]), (y, out.at[1, pl.ds(0, T)])]
    pairs += [(w_out.at[half], out.at[1, pl.ds(T, X * B)])]
    for j in range(X):
        pairs += [(w_in.at[:, columns(other, j)], out.at[0, pl.ds(T + j * B, B)])]
    copies = [pltpu.make_async_copy(a, b, sem.at[i]) for i, (a, b) in enumerate(pairs)]
    for copy in copies:
        copy.start()
    for copy in copies:
        copy.wait()


def partial_sums(x, w_in, y, w_out, theirs, out):
    core = this_core()
    for j in range(X):
        rows = slice(T + j * B, T + (j + 1) * B)
        h = dot(x[...], w_in[:, columns(core, j)], ((1,), (0,)))
        h = h + dot(theirs[0, :T], theirs[0, rows], ((1,), (0,)))
        g = dot(y[...], w_out[columns(core, j), :], ((1,), (1,)))
        g = g + dot(theirs[1, :T], theirs[1, rows], ((1,), (1,)))
        h, g = h.astype(BF16), g.astype(BF16)
        for z in range(Z):
            four, eight = place(core, j, z)
            out[four, eight, 0] = h[z * Q : (z + 1) * Q]
            out[four, eight, 1] = g[z * Q : (z + 1) * Q]


def total(parts):
    value = parts[0].astype(F32)
    for j in range(1, parts.shape[0]):
        value = value + parts[j].astype(F32)
    return value


def add_fours(parts, out):
    out[...] = total(parts).astype(BF16)


def middle(parts, out):
    both = total(parts)
    v, g = both[0], both[1]
    k = np.float32(np.sqrt(2 / np.pi))
    cube = np.float32(0.044715)
    t = jnp.tanh(k * (v + cube * (v * v * v)))
    act = (0.5 * v * (1.0 + t)).astype(BF16)
    slope = 0.5 * (1.0 + t) + 0.5 * v * (1.0 - t * t) * (
        k * (1.0 + 3.0 * cube * (v * v))
    )
    pre = (g * slope).astype(BF16)
    for j in range(X):
        out[j, 0] = act
        out[j, 1] = pre


def copies(part, out):
    for j in range(4):
        out[j] = part[...]


def tokens(ref, core, x, which):
    blocks = [ref[(*place(core, x, z), which)] for z in range(Z)]
    return jnp.concatenate(blocks, axis=0)


def input_part(mine, theirs, w, out):
    core = this_core()
    value = jnp.zeros((T, B), F32)
    for who, ref in ((core, mine), (1 - core, theirs)):
        for j in range(X):
            value += dot(tokens(ref, who, j, 1), w[:, columns(who, j)], ((1,), (1,)))
    out[...] = value


def weights(mine, theirs, x, y, out_in, out_out):
    core = this_core()
    for who, ref in ((core, mine), (1 - core, theirs)):
        for j in range(X):
            there = columns(who, j)
            out_in[:, there] = dot(x[...], tokens(ref, who, j, 1), ((0,), (0,)))
            out_out[there, :] = dot(tokens(ref, who, j, 0), y[...], ((0,), (0,)))


def finish(parts, out):
    out[...] = total(parts).astype(BF16)


def per_device(inputs, grad_out, w_in, w_out):
    s = jax.ShapeDtypeStruct
    swap = lambda v: lax.ppermute(v, "gx", SWAP)

    def exchange(v, groups):
        return lax.all_to_all(v, "gx", 0, 0, axis_index_groups=groups, tiled=True)

    both = (4, X, 2, Q, B)
    theirs = call(
        pack,
        s((2, T + X * B, B), BF16),
        *(inputs, w_in, grad_out, w_out),
        where=pltpu.HBM,
        params=pltpu.CompilerParams(vmem_limit_bytes=56 * 1024 * 1024),
        scratch=(pltpu.SemaphoreType.DMA((3 + X,)),),
    )
    theirs = swap(theirs)
    sums = call(partial_sums, s(both, BF16), inputs, w_in, grad_out, w_out, theirs)
    sums = call(add_fours, s(both[1:], BF16), exchange(sums, FOURS))
    mine = call(middle, s(both[1:], BF16), exchange(sums, EIGHTS))
    mine = exchange(call(copies, s(both, BF16), exchange(mine, EIGHTS)), FOURS)
    theirs = swap(mine)
    part = call(input_part, s((T, B), F32), mine, theirs, w_in)
    part = lax.all_to_all(part.reshape(16, T // 16, B), "gy", 0, 0, tiled=True)
    outs = (s((B, 2 * X * B), F32), s((2 * X * B, B), F32))
    grad_w_in, grad_w_out = call(weights, outs, mine, theirs, inputs, grad_out)
    grad_inputs = call(finish, s((T // 16, B), BF16), part)
    return (grad_inputs, grad_w_in, grad_w_out)


def solution(mesh):
    return jax.shard_map(
        per_device,
        mesh=mesh,
        in_specs=(P(None, "gx"), P(None, "gx"), P("gx", "gy"), P("gy", "gx")),
        out_specs=(P("gy", "gx"), P("gx", "gy"), P("gy", "gx")),
        check_vma=False,
    )
```

```python
import jax
import jax.numpy as jnp
import numpy as np
from jax import lax
from jax.experimental import pallas as pl
from jax.experimental.pallas import tpu as pltpu
from jax.sharding import PartitionSpec as P

F32, BF16 = jnp.float32, jnp.bfloat16
PARAMS = pltpu.CompilerParams(vmem_limit_bytes=40 * 1024 * 1024)
T, B = 384, 128
X, Z, C = 8, 4, 2
Q = T // Z

HALVES = ((0, 2, 3, 5), (7, 1, 4, 6))
at = lambda x, z, c: (x * Z + z) * C + c
FOURS = [[at(x, z, 0) for x in half] for half in HALVES for z in range(Z)]
FOURS += [[at(x, z, 1) for z in range(Z)] for x in range(X)]
EIGHTS = [[at(half[a], z, 0) for half in HALVES for z in range(Z)] for a in range(4)]
EIGHTS += [[at(x, z, 1) for x in range(X)] for z in range(Z)]
SWAP = [(i, i ^ 1) for i in range(X * Z * C)]


def place(core, x, z):
    first, half = core == 0, int(x in HALVES[1])
    return jnp.where(first, HALVES[half].index(x), z), jnp.where(first, half * Z + z, x)


def call(body, outs, *operands, where=pltpu.VMEM, params=PARAMS, scratch=()):
    vmem, read = (pl.BlockSpec(memory_space=m) for m in (pltpu.VMEM, where))
    return pl.pallas_call(
        body,
        out_shape=outs,
        in_specs=[read] * len(operands),
        out_specs=jax.tree.map(lambda _: vmem, outs),
        scratch_shapes=scratch,
        compiler_params=params,
    )(*operands)


def this_core():
    return lax.rem(lax.axis_index("gx"), C)


def columns(core, x):
    return pl.ds(pl.multiple_of((core * X + x) * B, B), B)


def dot(a, b, dims):
    return lax.dot_general(a, b, (dims, ((), ())), preferred_element_type=F32)


def pack(x, w_in, y, w_out, out, sem):
    other = 1 - this_core()
    half = pl.ds(pl.multiple_of(other * X * B, B), X * B)
    pairs = [(x, out.at[0, pl.ds(0, T)]), (y, out.at[1, pl.ds(0, T)])]
    pairs += [(w_out.at[half], out.at[1, pl.ds(T, X * B)])]
    for j in range(X):
        pairs += [(w_in.at[:, columns(other, j)], out.at[0, pl.ds(T + j * B, B)])]
    copies = [pltpu.make_async_copy(a, b, sem.at[i]) for i, (a, b) in enumerate(pairs)]
    for copy in copies:
        copy.start()
    for copy in copies:
        copy.wait()


def partial_sums(x, w_in, y, w_out, theirs, out):
    core = this_core()
    for j in range(X):
        rows = slice(T + j * B, T + (j + 1) * B)
        h = dot(x[...], w_in[:, columns(core, j)], ((1,), (0,)))
        h = h + dot(theirs[0, :T], theirs[0, rows], ((1,), (0,)))
        g = dot(y[...], w_out[columns(core, j), :], ((1,), (1,)))
        g = g + dot(theirs[1, :T], theirs[1, rows], ((1,), (1,)))
        h, g = h.astype(BF16), g.astype(BF16)
        for z in range(Z):
            four, eight = place(core, j, z)
            out[four, eight, 0] = h[z * Q : (z + 1) * Q]
            out[four, eight, 1] = g[z * Q : (z + 1) * Q]


def total(parts):
    value = parts[0].astype(F32)
    for j in range(1, parts.shape[0]):
        value = value + parts[j].astype(F32)
    return value


def add_fours(parts, out):
    out[...] = total(parts).astype(BF16)


def middle(parts, out):
    both = total(parts)
    v, g = both[0], both[1]
    k = np.float32(np.sqrt(2 / np.pi))
    cube = np.float32(0.044715)
    t = jnp.tanh(k * (v + cube * (v * v * v)))
    act = (0.5 * v * (1.0 + t)).astype(BF16)
    slope = 0.5 * (1.0 + t) + 0.5 * v * (1.0 - t * t) * (
        k * (1.0 + 3.0 * cube * (v * v))
    )
    pre = (g * slope).astype(BF16)
    for j in range(X):
        out[j, 0] = act
        out[j, 1] = pre


def copies(part, out):
    for j in range(4):
        out[j] = part[...]


def tokens(ref, core, x, which):
    blocks = [ref[(*place(core, x, z), which)] for z in range(Z)]
    return jnp.concatenate(blocks, axis=0)


def input_part(mine, theirs, w, out):
    core = this_core()
    value = jnp.zeros((T, B), F32)
    for who, ref in ((core, mine), (1 - core, theirs)):
        for j in range(X):
            value += dot(tokens(ref, who, j, 1), w[:, columns(who, j)], ((1,), (1,)))
    out[...] = value


def weights(mine, theirs, x, y, out_in, out_out):
    core = this_core()
    for who, ref in ((core, mine), (1 - core, theirs)):
        for j in range(X):
            there = columns(who, j)
            out_in[:, there] = dot(x[...], tokens(ref, who, j, 1), ((0,), (0,)))
            out_out[there, :] = dot(tokens(ref, who, j, 0), y[...], ((0,), (0,)))


def finish(parts, out):
    out[...] = total(parts).astype(BF16)


def per_device(inputs, grad_out, w_in, w_out):
    s = jax.ShapeDtypeStruct
    swap = lambda v: lax.ppermute(v, "gx", SWAP)

    def exchange(v, groups):
        return lax.all_to_all(v, "gx", 0, 0, axis_index_groups=groups, tiled=True)

    both = (4, X, 2, Q, B)
    theirs = call(
        pack,
        s((2, T + X * B, B), BF16),
        *(inputs, w_in, grad_out, w_out),
        where=pltpu.HBM,
        params=pltpu.CompilerParams(vmem_limit_bytes=56 * 1024 * 1024),
        scratch=(pltpu.SemaphoreType.DMA((3 + X,)),),
    )
    theirs = swap(theirs)
    sums = call(partial_sums, s(both, BF16), inputs, w_in, grad_out, w_out, theirs)
    sums = call(add_fours, s(both[1:], BF16), exchange(sums, FOURS))
    mine = call(middle, s(both[1:], BF16), exchange(sums, EIGHTS))
    mine = exchange(call(copies, s(both, BF16), exchange(mine, EIGHTS)), FOURS)
    theirs = swap(mine)
    part = call(input_part, s((T, B), F32), mine, theirs, w_in)
    part = lax.all_to_all(part.reshape(16, T // 16, B), "gy", 0, 0, tiled=True)
    outs = (s((B, 2 * X * B), F32), s((2 * X * B, B), F32))
    grad_w_in, grad_w_out = call(weights, outs, mine, theirs, inputs, grad_out)
    grad_inputs = call(finish, s((T // 16, B), BF16), part)
    return (grad_inputs, grad_w_in, grad_w_out)


def solution(mesh):
    return jax.shard_map(
        per_device,
        mesh=mesh,
        in_specs=(P(None, "gx"), P(None, "gx"), P("gx", "gy"), P("gy", "gx")),
        out_specs=(P("gy", "gx"), P("gx", "gy"), P("gy", "gx")),
        check_vma=False,
    )
```

```python
import jax
import jax.numpy as jnp
import numpy as np
from jax import lax
from jax.experimental import pallas as pl
from jax.experimental.pallas import tpu as pltpu
from jax.sharding import PartitionSpec as P

F32, BF16 = jnp.float32, jnp.bfloat16
PARAMS = pltpu.CompilerParams(vmem_limit_bytes=40 * 1024 * 1024)
T, B = 384, 128
X, Z, C = 8, 4, 2
Q = T // Z

HALVES = ((0, 2, 3, 5), (7, 1, 4, 6))
at = lambda x, z, c: (x * Z + z) * C + c


def groups(c):
    fours = [[at(x, z, c) for x in half] for half in HALVES for z in range(Z)]
    fours += [[at(x, z, 1 - c) for z in range(Z)] for x in range(X)]
    eights = [[at(half[a], z, c) for half in HALVES for z in range(Z)] for a in range(4)]
    eights += [[at(x, z, 1 - c) for x in range(X)] for z in range(Z)]
    return fours, eights


SWAP = [(i, i ^ 1) for i in range(X * Z * C)]


def place(first, x, z):
    half = int(x in HALVES[1])
    return jnp.where(first, HALVES[half].index(x), z), jnp.where(first, half * Z + z, x)


def call(body, outs, *operands, where=pltpu.VMEM, params=PARAMS, scratch=()):
    vmem, read = (pl.BlockSpec(memory_space=m) for m in (pltpu.VMEM, where))
    return pl.pallas_call(
        body,
        out_shape=outs,
        in_specs=[read] * len(operands),
        out_specs=jax.tree.map(lambda _: vmem, outs),
        scratch_shapes=scratch,
        compiler_params=params,
    )(*operands)


def this_core():
    return lax.rem(lax.axis_index("gx"), C)


def columns(core, x):
    return pl.ds(pl.multiple_of((core * X + x) * B, B), B)


def dot(a, b, dims):
    return lax.dot_general(a, b, (dims, ((), ())), preferred_element_type=F32)


def pack(x, w_in, y, w_out, out, sem):
    other = 1 - this_core()
    half = pl.ds(pl.multiple_of(other * X * B, B), X * B)
    pairs = [(x, out.at[0, pl.ds(0, T)]), (y, out.at[1, pl.ds(0, T)])]
    pairs += [(w_out.at[half], out.at[1, pl.ds(T, X * B)])]
    for j in range(X):
        pairs += [(w_in.at[:, columns(other, j)], out.at[0, pl.ds(T + j * B, B)])]
    copies = [pltpu.make_async_copy(a, b, sem.at[i]) for i, (a, b) in enumerate(pairs)]
    for copy in copies:
        copy.start()
    for copy in copies:
        copy.wait()


def partial_sums(x, w_in, y, w_out, theirs, out):
    core = this_core()
    for j in range(X):
        rows = slice(T + j * B, T + (j + 1) * B)
        h = dot(x[...], w_in[:, columns(core, j)], ((1,), (0,)))
        h = h + dot(theirs[0, :T], theirs[0, rows], ((1,), (0,)))
        g = dot(y[...], w_out[columns(core, j), :], ((1,), (1,)))
        g = g + dot(theirs[1, :T], theirs[1, rows], ((1,), (1,)))
        h, g = h.astype(BF16), g.astype(BF16)
        for z in range(Z):
            four, eight = place(core == 0, j, z)
            out[four, eight, 0] = h[z * Q : (z + 1) * Q]
            out[four, eight, 1] = g[z * Q : (z + 1) * Q]


def total(parts):
    value = parts[0].astype(F32)
    for j in range(1, parts.shape[0]):
        value = value + parts[j].astype(F32)
    return value


def add_fours(parts, out):
    out[...] = total(parts).astype(BF16)


def middle(parts, out):
    both = total(parts)
    v, g = both[0], both[1]
    k = np.float32(np.sqrt(2 / np.pi))
    cube = np.float32(0.044715)
    t = jnp.tanh(k * (v + cube * (v * v * v)))
    act = (0.5 * v * (1.0 + t)).astype(BF16)
    slope = 0.5 * (1.0 + t) + 0.5 * v * (1.0 - t * t) * (
        k * (1.0 + 3.0 * cube * (v * v))
    )
    pre = (g * slope).astype(BF16)
    for j in range(X):
        out[j, 0] = act
        out[j, 1] = pre


def copies(part, out):
    for j in range(4):
        out[j] = part[...]


def tokens(ref, core, x, which):
    blocks = [ref[(*place(core == 1, x, z), which)] for z in range(Z)]
    return jnp.concatenate(blocks, axis=0)


def input_part(mine, theirs, w, out):
    core = this_core()
    value = jnp.zeros((T, B), F32)
    for who, ref in ((core, mine), (1 - core, theirs)):
        for j in range(X):
            value += dot(tokens(ref, who, j, 1), w[:, columns(who, j)], ((1,), (1,)))
    out[...] = value


def weights(mine, theirs, x, y, out_in, out_out):
    core = this_core()
    for who, ref in ((core, mine), (1 - core, theirs)):
        for j in range(X):
            there = columns(who, j)
            out_in[:, there] = dot(x[...], tokens(ref, who, j, 1), ((0,), (0,)))
            out_out[there, :] = dot(tokens(ref, who, j, 0), y[...], ((0,), (0,)))


def finish(parts, out):
    out[...] = total(parts).astype(BF16)


def per_device(inputs, grad_out, w_in, w_out):
    s = jax.ShapeDtypeStruct
    swap = lambda v: lax.ppermute(v, "gx", SWAP)

    def exchange(v, groups):
        return lax.all_to_all(v, "gx", 0, 0, axis_index_groups=groups, tiled=True)

    both = (4, X, 2, Q, B)
    theirs = call(
        pack,
        s((2, T + X * B, B), BF16),
        *(inputs, w_in, grad_out, w_out),
        where=pltpu.HBM,
        params=pltpu.CompilerParams(vmem_limit_bytes=56 * 1024 * 1024),
        scratch=(pltpu.SemaphoreType.DMA((3 + X,)),),
    )
    theirs = swap(theirs)
    sums = call(partial_sums, s(both, BF16), inputs, w_in, grad_out, w_out, theirs)
    fours, eights = groups(0)
    sums = call(add_fours, s(both[1:], BF16), exchange(sums, fours))
    mine = call(middle, s(both[1:], BF16), exchange(sums, eights))
    fours, eights = groups(1)
    mine = exchange(call(copies, s(both, BF16), exchange(mine, eights)), fours)
    theirs = swap(mine)
    part = call(input_part, s((T, B), F32), mine, theirs, w_in)
    part = lax.all_to_all(part.reshape(16, T // 16, B), "gy", 0, 0, tiled=True)
    outs = (s((B, 2 * X * B), F32), s((2 * X * B, B), F32))
    grad_w_in, grad_w_out = call(weights, outs, mine, theirs, inputs, grad_out)
    grad_inputs = call(finish, s((T // 16, B), BF16), part)
    return (grad_inputs, grad_w_in, grad_w_out)


def solution(mesh):
    return jax.shard_map(
        per_device,
        mesh=mesh,
        in_specs=(P(None, "gx"), P(None, "gx"), P("gx", "gy"), P("gy", "gx")),
        out_specs=(P("gy", "gx"), P("gx", "gy"), P("gy", "gx")),
        check_vma=False,
    )
```

```python
import jax
import jax.numpy as jnp
import numpy as np
from jax import lax
from jax.experimental import pallas as pl
from jax.experimental.pallas import tpu as pltpu
from jax.sharding import PartitionSpec as P

F32, BF16 = jnp.float32, jnp.bfloat16
PARAMS = pltpu.CompilerParams(vmem_limit_bytes=40 * 1024 * 1024)
T, B = 384, 128
X, Z, C = 8, 4, 2
Q = T // Z

HALVES = ((0, 2, 3, 5), (7, 1, 4, 6))
at = lambda x, z, c: (x * Z + z) * C + c
FOURS = [[at(x, z, 0) for x in half] for half in HALVES for z in range(Z)]
FOURS += [[at(x, z, 1) for z in range(Z)] for x in range(X)]
EIGHTS = [[at(half[a], z, 0) for half in HALVES for z in range(Z)] for a in range(4)]
EIGHTS += [[at(x, z, 1) for x in range(X)] for z in range(Z)]
SWAP = [(i, i ^ 1) for i in range(X * Z * C)]


def place(core, x, z):
    first, half = core == 0, int(x in HALVES[1])
    return jnp.where(first, HALVES[half].index(x), z), jnp.where(first, half * Z + z, x)


def call(body, outs, *operands, unread=0, where=pltpu.VMEM, params=PARAMS, scratch=()):
    vmem, read, stay = (pl.BlockSpec(memory_space=m) for m in (pltpu.VMEM, where, pl.ANY))
    return pl.pallas_call(
        body,
        out_shape=outs,
        in_specs=[read] * (len(operands) - unread) + [stay] * unread,
        out_specs=jax.tree.map(lambda _: vmem, outs),
        scratch_shapes=scratch,
        compiler_params=params,
    )(*operands)


def this_core():
    return lax.rem(lax.axis_index("gx"), C)


def columns(core, x):
    return pl.ds(pl.multiple_of((core * X + x) * B, B), B)


def dot(a, b, dims):
    return lax.dot_general(a, b, (dims, ((), ())), preferred_element_type=F32)


def pack(x, w_in, y, w_out, out, sem):
    other = 1 - this_core()
    half = pl.ds(pl.multiple_of(other * X * B, B), X * B)
    pairs = [(x, out.at[0, pl.ds(0, T)]), (y, out.at[1, pl.ds(0, T)])]
    pairs += [(w_out.at[half], out.at[1, pl.ds(T, X * B)])]
    for j in range(X):
        pairs += [(w_in.at[:, columns(other, j)], out.at[0, pl.ds(T + j * B, B)])]
    copies = [pltpu.make_async_copy(a, b, sem.at[i]) for i, (a, b) in enumerate(pairs)]
    for copy in copies:
        copy.start()
    for copy in copies:
        copy.wait()


def partial_sums(x, w_in, y, w_out, theirs, out):
    core = this_core()
    for j in range(X):
        rows = slice(T + j * B, T + (j + 1) * B)
        h = dot(x[...], w_in[:, columns(core, j)], ((1,), (0,)))
        h = h + dot(theirs[0, :T], theirs[0, rows], ((1,), (0,)))
        g = dot(y[...], w_out[columns(core, j), :], ((1,), (1,)))
        g = g + dot(theirs[1, :T], theirs[1, rows], ((1,), (1,)))
        h, g = h.astype(BF16), g.astype(BF16)
        for z in range(Z):
            four, eight = place(core, j, z)
            out[four, eight, 0] = h[z * Q : (z + 1) * Q]
            out[four, eight, 1] = g[z * Q : (z + 1) * Q]


def total(parts):
    value = parts[0].astype(F32)
    for j in range(1, parts.shape[0]):
        value = value + parts[j].astype(F32)
    return value


def add_fours(parts, out):
    out[...] = total(parts).astype(BF16)


def middle(parts, out):
    both = total(parts)
    v, g = both[0], both[1]
    k = np.float32(np.sqrt(2 / np.pi))
    cube = np.float32(0.044715)
    t = jnp.tanh(k * (v + cube * (v * v * v)))
    act = (0.5 * v * (1.0 + t)).astype(BF16)
    slope = 0.5 * (1.0 + t) + 0.5 * v * (1.0 - t * t) * (
        k * (1.0 + 3.0 * cube * (v * v))
    )
    pre = (g * slope).astype(BF16)
    for j in range(X):
        out[j, 0] = act
        out[j, 1] = pre


def copies(part, out):
    for j in range(4):
        out[j] = part[...]


def tokens(ref, core, x, which):
    blocks = [ref[(*place(core, x, z), which)] for z in range(Z)]
    return jnp.concatenate(blocks, axis=0)


def input_parts(mine, w, theirs, own, other):
    core = this_core()
    here, there = jnp.zeros((T, B), F32), jnp.zeros((T, B), F32)
    for j in range(X):
        value = tokens(mine, core, j, 1)
        here += dot(value, w[:, columns(core, j)], ((1,), (1,)))
        there += dot(value, theirs[0, T + j * B : T + (j + 1) * B], ((1,), (1,)))
    own[...] = here
    other[...] = there


def weights(mine, theirs, x, y, out_in, out_out, done):
    core = this_core()
    done[...] = jnp.zeros_like(done)
    for who, ref in ((core, mine), (1 - core, theirs)):
        for j in range(X):
            there = columns(who, j)
            out_in[:, there] = dot(x[...], tokens(ref, who, j, 1), ((0,), (0,)))
            out_out[there, :] = dot(tokens(ref, who, j, 0), y[...], ((0,), (0,)))


def finish(parts, after, out):
    out[...] = total(parts).astype(BF16)


def per_device(inputs, grad_out, w_in, w_out):
    s = jax.ShapeDtypeStruct
    swap = lambda v: lax.ppermute(v, "gx", SWAP)

    def exchange(v, groups):
        return lax.all_to_all(v, "gx", 0, 0, axis_index_groups=groups, tiled=True)

    both = (4, X, 2, Q, B)
    theirs = call(
        pack,
        s((2, T + X * B, B), BF16),
        *(inputs, w_in, grad_out, w_out),
        where=pltpu.HBM,
        params=pltpu.CompilerParams(vmem_limit_bytes=56 * 1024 * 1024),
        scratch=(pltpu.SemaphoreType.DMA((3 + X,)),),
    )
    theirs = swap(theirs)
    sums = call(partial_sums, s(both, BF16), inputs, w_in, grad_out, w_out, theirs)
    sums = call(add_fours, s(both[1:], BF16), exchange(sums, FOURS))
    mine = call(middle, s(both[1:], BF16), exchange(sums, EIGHTS))
    mine = exchange(call(copies, s(both, BF16), exchange(mine, EIGHTS)), FOURS)
    own, other = call(input_parts, (s((T, B), F32),) * 2, mine, w_in, theirs)
    part = own + swap(other)
    part = lax.all_to_all(part.reshape(16, T // 16, B), "gy", 0, 0, tiled=True)
    theirs = swap(mine)
    outs = (s((B, 2 * X * B), F32), s((2 * X * B, B), F32), s((8, B), F32))
    grad_w_in, grad_w_out, done = call(weights, outs, mine, theirs, inputs, grad_out)
    grad_inputs = call(finish, s((T // 16, B), BF16), part, done, unread=1)
    return (grad_inputs, grad_w_in, grad_w_out)


def solution(mesh):
    return jax.shard_map(
        per_device,
        mesh=mesh,
        in_specs=(P(None, "gx"), P(None, "gx"), P("gx", "gy"), P("gy", "gx")),
        out_specs=(P("gy", "gx"), P("gx", "gy"), P("gy", "gx")),
        check_vma=False,
    )
```

```python
import jax
import jax.numpy as jnp
import numpy as np
from jax import lax
from jax.experimental import pallas as pl
from jax.experimental.pallas import tpu as pltpu
from jax.sharding import PartitionSpec as P

F32, BF16 = jnp.float32, jnp.bfloat16
PARAMS = pltpu.CompilerParams(vmem_limit_bytes=40 * 1024 * 1024)
T, B = 384, 128
X, Z, C = 8, 4, 2
Q = T // Z

HALVES = ((0, 2, 3, 5), (7, 1, 4, 6))
BACK = ((2, 4, 5, 7), (1, 3, 6, 0))
at = lambda x, z, c: (x * Z + z) * C + c


def groups(halves):
    fours = [[at(x, z, 0) for x in half] for half in halves for z in range(Z)]
    fours += [[at(x, z, 1) for z in range(Z)] for x in range(X)]
    eights = [[at(half[a], z, 0) for half in halves for z in range(Z)] for a in range(4)]
    eights += [[at(x, z, 1) for x in range(X)] for z in range(Z)]
    return fours, eights


SWAP = [(i, i ^ 1) for i in range(X * Z * C)]


def place(halves, core, x, z):
    first, half = core == 0, int(x in halves[1])
    return jnp.where(first, halves[half].index(x), z), jnp.where(first, half * Z + z, x)


def call(body, outs, *operands, where=pltpu.VMEM, params=PARAMS, scratch=()):
    vmem, read = (pl.BlockSpec(memory_space=m) for m in (pltpu.VMEM, where))
    return pl.pallas_call(
        body,
        out_shape=outs,
        in_specs=[read] * len(operands),
        out_specs=jax.tree.map(lambda _: vmem, outs),
        scratch_shapes=scratch,
        compiler_params=params,
    )(*operands)


def this_core():
    return lax.rem(lax.axis_index("gx"), C)


def columns(core, x):
    return pl.ds(pl.multiple_of((core * X + x) * B, B), B)


def dot(a, b, dims):
    return lax.dot_general(a, b, (dims, ((), ())), preferred_element_type=F32)


def pack(x, w_in, y, w_out, out, sem):
    other = 1 - this_core()
    half = pl.ds(pl.multiple_of(other * X * B, B), X * B)
    pairs = [(x, out.at[0, pl.ds(0, T)]), (y, out.at[1, pl.ds(0, T)])]
    pairs += [(w_out.at[half], out.at[1, pl.ds(T, X * B)])]
    for j in range(X):
        pairs += [(w_in.at[:, columns(other, j)], out.at[0, pl.ds(T + j * B, B)])]
    copies = [pltpu.make_async_copy(a, b, sem.at[i]) for i, (a, b) in enumerate(pairs)]
    for copy in copies:
        copy.start()
    for copy in copies:
        copy.wait()


def partial_sums(x, w_in, y, w_out, theirs, out):
    core = this_core()
    for j in range(X):
        rows = slice(T + j * B, T + (j + 1) * B)
        h = dot(x[...], w_in[:, columns(core, j)], ((1,), (0,)))
        h = h + dot(theirs[0, :T], theirs[0, rows], ((1,), (0,)))
        g = dot(y[...], w_out[columns(core, j), :], ((1,), (1,)))
        g = g + dot(theirs[1, :T], theirs[1, rows], ((1,), (1,)))
        h, g = h.astype(BF16), g.astype(BF16)
        for z in range(Z):
            four, eight = place(HALVES, core, j, z)
            out[four, eight, 0] = h[z * Q : (z + 1) * Q]
            out[four, eight, 1] = g[z * Q : (z + 1) * Q]


def total(parts):
    value = parts[0].astype(F32)
    for j in range(1, parts.shape[0]):
        value = value + parts[j].astype(F32)
    return value


def add_fours(parts, out):
    out[...] = total(parts).astype(BF16)


def middle(parts, out):
    both = total(parts)
    v, g = both[0], both[1]
    k = np.float32(np.sqrt(2 / np.pi))
    cube = np.float32(0.044715)
    t = jnp.tanh(k * (v + cube * (v * v * v)))
    act = (0.5 * v * (1.0 + t)).astype(BF16)
    slope = 0.5 * (1.0 + t) + 0.5 * v * (1.0 - t * t) * (
        k * (1.0 + 3.0 * cube * (v * v))
    )
    pre = (g * slope).astype(BF16)
    for j in range(X):
        out[j, 0] = act
        out[j, 1] = pre


def copies(part, out):
    for j in range(4):
        out[j] = part[...]


def tokens(ref, core, x, which):
    blocks = [ref[(*place(BACK, core, x, z), which)] for z in range(Z)]
    return jnp.concatenate(blocks, axis=0)


def input_part(mine, theirs, w, out):
    core = this_core()
    value = jnp.zeros((T, B), F32)
    for who, ref in ((core, mine), (1 - core, theirs)):
        for j in range(X):
            value += dot(tokens(ref, who, j, 1), w[:, columns(who, j)], ((1,), (1,)))
    out[...] = value


def weights(mine, theirs, x, y, out_in, out_out):
    core = this_core()
    for who, ref in ((core, mine), (1 - core, theirs)):
        for j in range(X):
            there = columns(who, j)
            out_in[:, there] = dot(x[...], tokens(ref, who, j, 1), ((0,), (0,)))
            out_out[there, :] = dot(tokens(ref, who, j, 0), y[...], ((0,), (0,)))


def finish(parts, out):
    out[...] = total(parts).astype(BF16)


def per_device(inputs, grad_out, w_in, w_out):
    s = jax.ShapeDtypeStruct
    swap = lambda v: lax.ppermute(v, "gx", SWAP)

    def exchange(v, groups):
        return lax.all_to_all(v, "gx", 0, 0, axis_index_groups=groups, tiled=True)

    both = (4, X, 2, Q, B)
    theirs = call(
        pack,
        s((2, T + X * B, B), BF16),
        *(inputs, w_in, grad_out, w_out),
        where=pltpu.HBM,
        params=pltpu.CompilerParams(vmem_limit_bytes=56 * 1024 * 1024),
        scratch=(pltpu.SemaphoreType.DMA((3 + X,)),),
    )
    theirs = swap(theirs)
    sums = call(partial_sums, s(both, BF16), inputs, w_in, grad_out, w_out, theirs)
    fours, eights = groups(HALVES)
    sums = call(add_fours, s(both[1:], BF16), exchange(sums, fours))
    mine = call(middle, s(both[1:], BF16), exchange(sums, eights))
    fours, eights = groups(BACK)
    mine = exchange(call(copies, s(both, BF16), exchange(mine, eights)), fours)
    theirs = swap(mine)
    part = call(input_part, s((T, B), F32), mine, theirs, w_in)
    part = lax.all_to_all(part.reshape(16, T // 16, B), "gy", 0, 0, tiled=True)
    outs = (s((B, 2 * X * B), F32), s((2 * X * B, B), F32))
    grad_w_in, grad_w_out = call(weights, outs, mine, theirs, inputs, grad_out)
    grad_inputs = call(finish, s((T // 16, B), BF16), part)
    return (grad_inputs, grad_w_in, grad_w_out)


def solution(mesh):
    return jax.shard_map(
        per_device,
        mesh=mesh,
        in_specs=(P(None, "gx"), P(None, "gx"), P("gx", "gy"), P("gy", "gx")),
        out_specs=(P("gy", "gx"), P("gx", "gy"), P("gy", "gx")),
        check_vma=False,
    )
```

```python
import jax
import jax.numpy as jnp
import numpy as np
from jax import lax
from jax.experimental import pallas as pl
from jax.experimental.pallas import tpu as pltpu
from jax.sharding import PartitionSpec as P

F32, BF16 = jnp.float32, jnp.bfloat16
PARAMS = pltpu.CompilerParams(vmem_limit_bytes=40 * 1024 * 1024)
T, B = 384, 128
X, Z, C = 8, 4, 2
Q = T // Z

HALVES = ((0, 2, 3, 5), (7, 1, 4, 6))
BACK = ((0, 1, 2, 3), (7, 6, 5, 4))
at = lambda x, z, c: (x * Z + z) * C + c


def groups(halves):
    fours = [[at(x, z, 0) for x in half] for half in halves for z in range(Z)]
    fours += [[at(x, z, 1) for z in range(Z)] for x in range(X)]
    eights = [[at(half[a], z, 0) for half in halves for z in range(Z)] for a in range(4)]
    eights += [[at(x, z, 1) for x in range(X)] for z in range(Z)]
    return fours, eights


SWAP = [(i, i ^ 1) for i in range(X * Z * C)]


def place(halves, core, x, z):
    first, half = core == 0, int(x in halves[1])
    return jnp.where(first, halves[half].index(x), z), jnp.where(first, half * Z + z, x)


def call(body, outs, *operands, where=pltpu.VMEM, params=PARAMS, scratch=()):
    vmem, read = (pl.BlockSpec(memory_space=m) for m in (pltpu.VMEM, where))
    return pl.pallas_call(
        body,
        out_shape=outs,
        in_specs=[read] * len(operands),
        out_specs=jax.tree.map(lambda _: vmem, outs),
        scratch_shapes=scratch,
        compiler_params=params,
    )(*operands)


def this_core():
    return lax.rem(lax.axis_index("gx"), C)


def columns(core, x):
    return pl.ds(pl.multiple_of((core * X + x) * B, B), B)


def dot(a, b, dims):
    return lax.dot_general(a, b, (dims, ((), ())), preferred_element_type=F32)


def pack(x, w_in, y, w_out, out, sem):
    other = 1 - this_core()
    half = pl.ds(pl.multiple_of(other * X * B, B), X * B)
    pairs = [(x, out.at[0, pl.ds(0, T)]), (y, out.at[1, pl.ds(0, T)])]
    pairs += [(w_out.at[half], out.at[1, pl.ds(T, X * B)])]
    for j in range(X):
        pairs += [(w_in.at[:, columns(other, j)], out.at[0, pl.ds(T + j * B, B)])]
    copies = [pltpu.make_async_copy(a, b, sem.at[i]) for i, (a, b) in enumerate(pairs)]
    for copy in copies:
        copy.start()
    for copy in copies:
        copy.wait()


def partial_sums(x, w_in, y, w_out, theirs, out):
    core = this_core()
    for j in range(X):
        rows = slice(T + j * B, T + (j + 1) * B)
        h = dot(x[...], w_in[:, columns(core, j)], ((1,), (0,)))
        h = h + dot(theirs[0, :T], theirs[0, rows], ((1,), (0,)))
        g = dot(y[...], w_out[columns(core, j), :], ((1,), (1,)))
        g = g + dot(theirs[1, :T], theirs[1, rows], ((1,), (1,)))
        h, g = h.astype(BF16), g.astype(BF16)
        for z in range(Z):
            four, eight = place(HALVES, core, j, z)
            out[four, eight, 0] = h[z * Q : (z + 1) * Q]
            out[four, eight, 1] = g[z * Q : (z + 1) * Q]


def total(parts):
    value = parts[0].astype(F32)
    for j in range(1, parts.shape[0]):
        value = value + parts[j].astype(F32)
    return value


def add_fours(parts, out):
    out[...] = total(parts).astype(BF16)


def middle(parts, out):
    both = total(parts)
    v, g = both[0], both[1]
    k = np.float32(np.sqrt(2 / np.pi))
    cube = np.float32(0.044715)
    t = jnp.tanh(k * (v + cube * (v * v * v)))
    act = (0.5 * v * (1.0 + t)).astype(BF16)
    slope = 0.5 * (1.0 + t) + 0.5 * v * (1.0 - t * t) * (
        k * (1.0 + 3.0 * cube * (v * v))
    )
    pre = (g * slope).astype(BF16)
    for j in range(X):
        out[j, 0] = act
        out[j, 1] = pre


def copies(part, out):
    for j in range(4):
        out[j] = part[...]


def tokens(ref, core, x, which):
    blocks = [ref[(*place(BACK, core, x, z), which)] for z in range(Z)]
    return jnp.concatenate(blocks, axis=0)


def input_part(mine, theirs, w, out):
    core = this_core()
    value = jnp.zeros((T, B), F32)
    for who, ref in ((core, mine), (1 - core, theirs)):
        for j in range(X):
            value += dot(tokens(ref, who, j, 1), w[:, columns(who, j)], ((1,), (1,)))
    out[...] = value


def weights(mine, theirs, x, y, out_in, out_out):
    core = this_core()
    for who, ref in ((core, mine), (1 - core, theirs)):
        for j in range(X):
            there = columns(who, j)
            out_in[:, there] = dot(x[...], tokens(ref, who, j, 1), ((0,), (0,)))
            out_out[there, :] = dot(tokens(ref, who, j, 0), y[...], ((0,), (0,)))


def finish(parts, out):
    out[...] = total(parts).astype(BF16)


def per_device(inputs, grad_out, w_in, w_out):
    s = jax.ShapeDtypeStruct
    swap = lambda v: lax.ppermute(v, "gx", SWAP)

    def exchange(v, groups):
        return lax.all_to_all(v, "gx", 0, 0, axis_index_groups=groups, tiled=True)

    both = (4, X, 2, Q, B)
    theirs = call(
        pack,
        s((2, T + X * B, B), BF16),
        *(inputs, w_in, grad_out, w_out),
        where=pltpu.HBM,
        params=pltpu.CompilerParams(vmem_limit_bytes=56 * 1024 * 1024),
        scratch=(pltpu.SemaphoreType.DMA((3 + X,)),),
    )
    theirs = swap(theirs)
    sums = call(partial_sums, s(both, BF16), inputs, w_in, grad_out, w_out, theirs)
    fours, eights = groups(HALVES)
    sums = call(add_fours, s(both[1:], BF16), exchange(sums, fours))
    mine = call(middle, s(both[1:], BF16), exchange(sums, eights))
    fours, eights = groups(BACK)
    mine = exchange(call(copies, s(both, BF16), exchange(mine, eights)), fours)
    theirs = swap(mine)
    part = call(input_part, s((T, B), F32), mine, theirs, w_in)
    part = lax.all_to_all(part.reshape(16, T // 16, B), "gy", 0, 0, tiled=True)
    outs = (s((B, 2 * X * B), F32), s((2 * X * B, B), F32))
    grad_w_in, grad_w_out = call(weights, outs, mine, theirs, inputs, grad_out)
    grad_inputs = call(finish, s((T // 16, B), BF16), part)
    return (grad_inputs, grad_w_in, grad_w_out)


def solution(mesh):
    return jax.shard_map(
        per_device,
        mesh=mesh,
        in_specs=(P(None, "gx"), P(None, "gx"), P("gx", "gy"), P("gy", "gx")),
        out_specs=(P("gy", "gx"), P("gx", "gy"), P("gy", "gx")),
        check_vma=False,
    )
```
